256 devices in a mesh: stream: 32 (over y, z_lo, x), span: 8 (over z_hi, core).
Axes of the slice: x: 4, y: 4, z: 8 (z_hi: 4, z_lo: 2; z = z_hi * 2 + z_lo), core: 2. Of those that a mesh axis runs over, the one named last changes fastest.
Arguments:
- adjoint_start: float32 [5, 256, 128, 512], P(None, 'stream', 'span'), may hold values from -4 to 4
- source: float32 [5, 256, 128, 512], P(None, 'stream', 'span'), may hold values from -40 to 40
- flow_state: float32 [5, 256, 128, 512], P(None, 'stream', 'span'), may hold values from -4 to 4, as said below
- precond: float32 [5, 5, 256, 128, 512], P(None, None, 'stream', 'span'), may hold values from -0.12 to 0.2
- flux_jac: float32 [3, 5, 5], replicated, may hold values from -4 to 4
- bc_codes: int32 [256, 128], P('stream', 'span'), may hold values from 0 to 2
Outputs:
- adjoint: float32 [5, 256, 128, 512], P(None, 'stream', 'span')
- residual_rms: float32 [2], replicated
The draws below stay inside these ranges and needn't reach their ends.
Inputs may be any that keep to these rules, and one draw needn't show every extreme that they name: `bc_codes`: 0 is a wall, 1 a far field, 2 an extrapolation face. `flow_state`: density and pressure lie in 0.5 to 2.
All inputs are finite; a program needn't handle non-finite values.
Results may differ from the reference program's by a relative error of at most 0.0003.
Values sent between devices are 32-bit elements; how exact they have to be, the bound alone decides.
A program may use at most 128 MiB of HBM per device.

```python
import jax
import jax.numpy as jnp
from jax import lax

NV = 5
SWEEPS = 2
NI = 256
NJ = 128
NK = 512


def draw_flow_state(key, part):
    keys = jax.random.split(key, 3)
    density = jax.random.uniform(keys[0], (1, NI, NJ, NK), jnp.float32, 0.5, 2.0)
    momentum = jax.random.truncated_normal(keys[1], -4.0, 4.0, (3, NI, NJ, NK), jnp.float32)
    pressure = jax.random.uniform(keys[2], (1, NI, NJ, NK), jnp.float32, 0.5, 2.0)
    return jnp.concatenate([density, momentum, pressure], axis=0)


def draw_source(key, part):
    keys = jax.random.split(key, 2)
    ramp = 10.0 ** (jnp.arange(NI, dtype=jnp.float32) / (NI - 1))
    column = 10.0 ** jax.random.uniform(keys[1], (NJ,), jnp.float32, 0.0, 1.0)
    base = jax.random.truncated_normal(keys[0], -4.0, 4.0, (NV, NI, NJ, NK), jnp.float32)
    return 0.1 * base * ramp[None, :, None, None] * column[None, None, :, None]


def draw_precond(key, part):
    keys = jax.random.split(key, 2)
    diagonal = jax.random.uniform(keys[0], (NV, NI, NJ, NK), jnp.float32, 0.08, 0.2)
    offdiag = 0.03 * jax.random.truncated_normal(keys[1], -4.0, 4.0, (NV, NV, NI, NJ, NK), jnp.float32)
    identity = jnp.eye(NV, dtype=jnp.float32)[:, :, None, None, None]
    return offdiag * (1.0 - identity) + identity * diagonal[:, None]


def set_ends(result, own_key, least, high):
    dims = result.shape
    spot = [jax.random.randint(jax.random.fold_in(own_key, axis), (), 0, dims[axis]) for axis in range(len(dims))]
    result = result.at[tuple(spot)].set(least)
    longest = dims.index(max(dims))
    spot[longest] = (spot[longest] + 1) % dims[longest]
    return result.at[tuple(spot)].set(high)


def levels(rng, extent, cuts, low, largest):
    def one(dim, blocks):
        steps = jax.random.uniform(jax.random.fold_in(jax.random.fold_in(rng, 6), dim), (blocks,), jnp.float32, low / len(cuts), largest / len(cuts))
        return jnp.repeat(jnp.exp(steps), extent[dim] // blocks).reshape((-1,) + (1,) * (len(extent) - dim - 1))

    level = one(*cuts[0])
    for cut in cuts[1:]:
        level = level * one(*cut)
    return level


def noise(key, shape, spread, limit, pieces=(), kind=jnp.bfloat16):
    entries = spread * jax.random.normal(key, shape, jnp.float32)
    if pieces:
        entries = entries * levels(key, shape, pieces, -0.22, 0.18)
    return jnp.clip(entries, -limit, limit).astype(kind)


def setup_inputs(seed: int = 0) -> dict:
    key_of = jax.random.split(jax.random.key(seed), 7)
    adjoint_start = noise(key_of[0], (NV, NI, NJ, NK), 0.3, 4.0, ((1, 32), (2, 8)), jnp.float32)
    source = draw_source(jax.random.fold_in(key_of[6], 71), 0)
    flow_state = draw_flow_state(jax.random.fold_in(key_of[6], 71), 0)
    precond = draw_precond(jax.random.fold_in(key_of[6], 71), 0)
    flux_jac = noise(key_of[4], (3, NV, NV), 0.3, 4.0, (), jnp.float32)
    bc_codes = set_ends(jax.random.randint(key_of[5], (NI, NJ), 0, 3), jax.random.fold_in(key_of[5], 1), 0, 2).astype(jnp.int32)
    return dict(adjoint_start=adjoint_start, source=source, flow_state=flow_state, precond=precond, flux_jac=flux_jac, bc_codes=bc_codes)


def transposed(jacobian, jump):
    return jnp.einsum('uv,u...->v...', jacobian, jump, precision=lax.Precision.HIGHEST)

def face_terms(left_side, right_side, speed_left, speed_right, jacobian):
    jump = left_side - right_side
    spectral = 0.5 * (speed_left + speed_right)
    central = 0.5 * transposed(jacobian, jump)
    upwind = 0.5 * spectral[None] * jump
    return (central + upwind, central - upwind)

def axis_term(adjoint_pad, speed_padded, jacobian, axis_dim):
    planes = adjoint_pad.shape[axis_dim] - 2
    to_left, to_right = face_terms(lax.slice_in_dim(adjoint_pad, 0, planes + 1, axis=axis_dim), lax.slice_in_dim(adjoint_pad, 1, planes + 2, axis=axis_dim), lax.slice_in_dim(speed_padded, 0, planes + 1, axis=axis_dim - 1), lax.slice_in_dim(speed_padded, 1, planes + 2, axis=axis_dim - 1), jacobian)
    return lax.slice_in_dim(to_left, 1, planes + 1, axis=axis_dim) + lax.slice_in_dim(to_right, 0, planes, axis=axis_dim)

def wall_term(adjoint, speeds, jacobian, bc_codes):
    bottom = adjoint[:, :, :, 0]
    signs = jnp.array([1.0, 1.0, 1.0, -1.0, 1.0], dtype=jnp.float32)[:, None, None]
    factor = jnp.where((bc_codes == 0)[None], signs, jnp.where((bc_codes == 2)[None], 1.0, 0.0)).astype(jnp.float32)
    return -factor * (0.5 * transposed(jacobian, bottom) + 0.25 * speeds[None, :, :, 0] * bottom)

def speeds_of(flow_state):
    density = flow_state[0]
    momentum = flow_state[1:4]
    pressure = flow_state[4]
    return jnp.sqrt(lax.optimization_barrier(jnp.sum(momentum * momentum, axis=0))) / density + jnp.sqrt(1.4 * pressure / density)

def precondition(precond, residual):
    total = precond[0] * residual[0]
    for row_index in range(1, 5):
        total = total + precond[row_index] * residual[row_index]
    return total

def adjoint_operator(adjoint, speeds, flux_jac, bc_codes):
    total = axis_term(jnp.pad(adjoint, ((0, 0), (1, 1), (0, 0), (0, 0))), jnp.pad(speeds, ((1, 1), (0, 0), (0, 0))), flux_jac[0], 1)
    total = total + axis_term(jnp.pad(adjoint, ((0, 0), (0, 0), (1, 1), (0, 0))), jnp.pad(speeds, ((0, 0), (1, 1), (0, 0))), flux_jac[1], 2)
    total = total + axis_term(jnp.pad(adjoint, ((0, 0), (0, 0), (0, 0), (1, 1))), jnp.pad(speeds, ((0, 0), (0, 0), (1, 1))), flux_jac[2], 3)
    bottom = wall_term(adjoint, speeds, flux_jac[2], bc_codes)
    return jnp.concatenate([total[..., :1] + bottom[..., None], total[..., 1:]], axis=3)

def reference(adjoint_start, source, flow_state, precond, flux_jac, bc_codes):
    speeds = speeds_of(flow_state)
    adjoint = adjoint_start
    rms_list = []
    for sweep_index in range(SWEEPS):
        residual = source - adjoint_operator(adjoint, speeds, flux_jac, bc_codes)
        rms_list.append(jnp.sqrt(jnp.sum(residual * residual) / residual.size))
        adjoint = adjoint + precondition(precond, residual)
    return (adjoint, jnp.stack(rms_list))
```

```python
import functools

import jax
import jax.numpy as jnp
from jax import lax
from jax.experimental import pallas as pl
from jax.experimental.pallas import tpu as pltpu
from jax.sharding import PartitionSpec as P

MESH = pl.DeviceIdType.MESH
NV = 5
J0 = 8


def ring(value, step, size):
    return lax.rem(value + step, size)


def reduction_partners(stream, span):
    y, z_lo, x = stream // 8, lax.rem(stream // 4, 2), lax.rem(stream, 4)
    z_hi, core = span // 2, lax.rem(span, 2)

    def at(dy, dl, dx, dh, dc):
        line = ring(y, dy, 4) * 8 + ring(z_lo, dl, 2) * 4 + ring(x, dx, 4)
        return (line, ring(z_hi, dh, 4) * 2 + ring(core, dc, 2))

    far = (2, 1, 3, 0)
    first = [(0, dl, 0, dh, dc) for dh in far for dl in (1, 0) for dc in (1, 0)]
    order = sorted(((dy, dx) for dy in range(4) for dx in range(4)), key=lambda d: -sum(min(t, 4 - t) for t in d))
    second = [(dy, 0, dx, 0, 0) for dy, dx in order]
    return [[at(*step) for step in steps if any(step)] for steps in (first, second)]


def kernel(
    cells_all, start_ref, source_ref, flow_ref, precond_ref, jac_ref, codes_ref, out, rms_ref,
    v0, v1, speed, flow, source, precond, jac, codes, ghost, flip, part, gathered,
    load_sem, i_send, i_recv, j_send, j_recv, s_send, s_recv, r_send, r_recv,
):
    stream, span = lax.axis_index("stream"), lax.axis_index("span")
    streams, spans = lax.axis_size("stream"), lax.axis_size("span")
    ni, nj, nk = flow.shape[1:]
    chunks = nk // 128
    rows = pl.ds(J0, nj)

    i_side = [(stream > 0, (stream - 1, span)), (stream < streams - 1, (stream + 1, span))]
    j_side = [(span > 0, (stream, span - 1)), (span < spans - 1, (stream, span + 1))]
    stages = reduction_partners(stream, span)

    barrier = pltpu.get_barrier_semaphore()
    for there, device in i_side + j_side:

        @pl.when(there)
        def _():
            pl.semaphore_signal(barrier, inc=1, device_id=device, device_id_type=MESH)

    for device in stages[0] + stages[1]:
        pl.semaphore_signal(barrier, inc=1, device_id=device, device_id_type=MESH)

    load_flow = pltpu.make_async_copy(flow_ref, flow, load_sem.at[0])
    load_start = [
        pltpu.make_async_copy(
            start_ref.at[:, :, :, pl.ds(128 * c, 128)], v0.at[:, pl.ds(1, ni), c, rows, :], load_sem.at[1 + c]
        )
        for c in range(chunks)
    ]
    load_source = pltpu.make_async_copy(source_ref, source, load_sem.at[1 + chunks])
    load_precond = [
        pltpu.make_async_copy(precond_ref.at[u], precond.at[u], load_sem.at[2 + chunks + u]) for u in range(NV)
    ]
    load_jac = pltpu.make_async_copy(jac_ref, jac, load_sem.at[2 + chunks + NV])
    load_codes = pltpu.make_async_copy(codes_ref, codes, load_sem.at[3 + chunks + NV])
    for copy in [load_codes, load_jac, load_flow, *load_start, load_source, *load_precond]:
        copy.start()

    def halo_i(buffer, sweep, side, first, count, source_of=None):
        own, other = (1, ni + 1) if side == 0 else (ni, 0)
        if source_of is None:
            lead = slice(None), own, pl.ds(first, count), rows, slice(None)
            src = buffer.at[lead]
            dst = buffer.at[:, other, pl.ds(first, count), rows, :]
        else:
            src = source_of.at[:, own - 1, :, pl.ds(128 * first, 128)]
            dst = buffer.at[:, other, first, rows, :]
        return pltpu.make_async_remote_copy(
            src_ref=src, dst_ref=dst, send_sem=i_send.at[sweep, side, first],
            recv_sem=i_recv.at[sweep, 1 - side, first], device_id=i_side[side][1], device_id_type=MESH,
        )

    def halo_j(buffer, piece, side, first, count):
        own, other = (J0, J0 + nj) if side == 0 else (J0 + nj - 1, J0 - 1)
        planes = pl.ds(1 + first, count)
        return pltpu.make_async_remote_copy(
            src_ref=buffer.at[:, planes, :, pl.ds(own, 1), :], dst_ref=buffer.at[:, planes, :, pl.ds(other, 1), :],
            send_sem=j_send.at[piece, side], recv_sem=j_recv.at[piece, 1 - side],
            device_id=j_side[side][1], device_id_type=MESH,
        )

    def halo_speed(axis, side):
        if axis == 0:
            own, other = (1, ni + 1) if side == 0 else (ni, 0)
            src, dst = speed.at[own, :, rows, :], speed.at[other, :, rows, :]
            device = i_side[side][1]
        else:
            own, other = (J0, J0 + nj) if side == 0 else (J0 + nj - 1, J0 - 1)
            planes = pl.ds(1, ni)
            src, dst = speed.at[planes, :, pl.ds(own, 1), :], speed.at[planes, :, pl.ds(other, 1), :]
            device = j_side[side][1]
        return pltpu.make_async_remote_copy(
            src_ref=src, dst_ref=dst, send_sem=s_send.at[axis, side], recv_sem=s_recv.at[axis, 1 - side],
            device_id=device, device_id_type=MESH,
        )

    def on_sides(sides, make, act):
        for side in (0, 1):

            @pl.when(sides[side][0])
            def _():
                act(make, side)

    def start(make, side):
        make(side).start()

    def arrived(make, side):
        make(1 - side).wait_recv()

    def sent(make, side):
        make(side).wait_send()

    zero_plane = jnp.zeros((chunks, nj, 128), jnp.float32)
    zero_rows = jnp.zeros((1, 128), jnp.float32)
    for side in (0, 1):
        plane, row = (0, J0 - 1) if side == 0 else (ni + 1, J0 + nj)

        @pl.when(jnp.logical_not(i_side[side][0]))
        def _():
            speed[plane, :, rows, :] = zero_plane
            for u in range(NV):
                v0[u, plane, :, rows, :] = zero_plane
                v1[u, plane, :, rows, :] = zero_plane

        @pl.when(jnp.logical_not(j_side[side][0]))
        def _():
            def clear(i, carry):
                for c in range(chunks):
                    speed[i + 1, c, pl.ds(row, 1), :] = zero_rows
                    for u in range(NV):
                        v0[u, i + 1, c, pl.ds(row, 1), :] = zero_rows
                        v1[u, i + 1, c, pl.ds(row, 1), :] = zero_rows
                return carry

            lax.fori_loop(0, ni, clear, 0)

    lane = lax.broadcasted_iota(jnp.int32, (nj, 128), 1)
    diagonal = lax.broadcasted_iota(jnp.int32, (nj, nj), 0) == lax.broadcasted_iota(jnp.int32, (nj, nj), 1)
    load_codes.wait()
    for i in range(ni):
        line = jnp.broadcast_to(codes[i : i + 1, :].astype(jnp.float32), (nj, nj))
        column = jnp.sum(jnp.where(diagonal, line, 0.0), axis=1, keepdims=True)
        column = jnp.broadcast_to(column, (nj, 128))
        ghost[i] = jnp.where(column == 1.0, 0.0, -1.0)
        flip[i] = jnp.where((column == 0.0) & (lane == 0), 2.0, 0.0)

    peers = sum(len(stage) for stage in stages)
    for there, _ in i_side + j_side:
        peers = peers + jnp.where(there, 1, 0)
    pl.semaphore_wait(barrier, peers)

    for c in range(chunks):
        on_sides(i_side, lambda side: halo_i(v0, 0, side, c, 1, start_ref), start)

    load_flow.wait()

    def speeds(i):
        density = flow[0, i]
        momentum = flow[1, i] * flow[1, i] + flow[2, i] * flow[2, i] + flow[3, i] * flow[3, i]
        quarter = 0.25 * (jnp.sqrt(momentum) / density + jnp.sqrt(1.4 * flow[4, i] / density))
        for c in range(chunks):
            speed[i + 1, c, rows, :] = quarter[:, 128 * c : 128 * c + 128]

    def loop_speeds(first, count, stride):
        def step(t, carry):
            speeds(first + stride * t)
            return carry

        lax.fori_loop(0, count, step, 0)

    loop_speeds(0, 2, ni - 1)
    on_sides(i_side, functools.partial(halo_speed, 0), start)
    for copy in load_start:
        copy.wait()
    on_sides(j_side, lambda side: halo_j(v0, 0, side, 0, ni), start)
    loop_speeds(1, ni - 2, 1)
    on_sides(j_side, functools.partial(halo_speed, 1), start)

    load_jac.wait()
    half = [[[0.5 * jac[u, d, v] for v in range(NV)] for u in range(NV)] for d in range(3)]

    def along_k(read, h, mirror):
        own = [read(2 * h), read(2 * h + 1)]
        up = [pltpu.roll(x, 1, 1) for x in own]
        down = [pltpu.roll(x, 127, 1) for x in own]
        before = mirror * own[0] if h == 0 else pltpu.roll(read(2 * h - 1), 1, 1)
        after = jnp.zeros_like(own[0]) if 2 * h + 2 == chunks else pltpu.roll(read(2 * h + 2), 127, 1)
        first, last = lane == 0, lane == 127
        left = [jnp.where(first, before, up[0]), jnp.where(first, up[0], up[1])]
        right = [jnp.where(last, down[1], down[0]), jnp.where(last, after, down[1])]
        return own, left, right

    def update(v, i, h, store):
        mirror = ghost[i]
        s_own, s_left, s_right = along_k(lambda c: speed[i + 1, c, rows, :], h, mirror)
        around = [along_k(lambda c, u=u: v[u, i + 1, c, rows, :], h, mirror) for u in range(NV)]
        squares = jnp.zeros((nj, 128), jnp.float32)
        for q in (0, 1):
            c = 2 * h + q
            own = [around[u][0][q] for u in range(NV)]
            s = s_own[q]
            places = [
                (speed[i, c, rows, :], lambda u, c=c: v[u, i, c, rows, :]),
                (speed[i + 2, c, rows, :], lambda u, c=c: v[u, i + 2, c, rows, :]),
                (speed[i + 1, c, pl.ds(J0 - 1, nj), :], lambda u, c=c: v[u, i + 1, c, pl.ds(J0 - 1, nj), :]),
                (speed[i + 1, c, pl.ds(J0 + 1, nj), :], lambda u, c=c: v[u, i + 1, c, pl.ds(J0 + 1, nj), :]),
                (s_left[q], lambda u, q=q: around[u][1][q]),
                (s_right[q], lambda u, q=q: around[u][2][q]),
            ]
            weights = [s + beside for beside, _ in places]
            total = functools.reduce(jnp.add, weights)
            r = [source[u, i, :, 128 * c : 128 * c + 128] - total * own[u] for u in range(NV)]
            for d in range(3):
                jump = []
                for u in range(NV):
                    low, high = places[2 * d][1](u), places[2 * d + 1][1](u)
                    r[u] = r[u] + (weights[2 * d] * low + weights[2 * d + 1] * high)
                    jump.append(high - low)
                for w in range(NV):
                    for u in range(NV):
                        r[w] = r[w] + half[d][u][w] * jump[u]
            if c == 0:
                wall = s * own[3]
                for u in range(NV):
                    wall = wall + half[2][u][3] * own[u]
                r[3] = r[3] - flip[i] * wall
            for w in range(NV):
                new = own[w]
                for u in range(NV):
                    new = new + precond[u, w, i, :, 128 * c : 128 * c + 128] * r[u]
                store(w, c, new)
                squares = squares + r[w] * r[w]
        return squares

    def planes(v, first, count, stride, halves, store, squares):
        def step(t, carry):
            i = first + stride * t
            for h in halves:
                carry = carry + update(v, i, h, functools.partial(store, i))
            return carry

        return lax.fori_loop(0, count, step, squares)

    def store_v1(i, w, c, new):
        v1[w, i + 1, c, rows, :] = new

    def store_out(i, w, c, new):
        out[w, i, :, 128 * c : 128 * c + 128] = new

    load_source.wait()
    for copy in load_precond:
        copy.wait()

    none = jnp.zeros((nj, 128), jnp.float32)
    halves = tuple(range(chunks // 2))

    on_sides(j_side, functools.partial(halo_speed, 1), arrived)
    on_sides(j_side, lambda side: halo_j(v0, 0, side, 0, ni), arrived)
    squares0 = planes(v0, 1, ni - 2, 1, halves, store_v1, none)
    inner_j = lambda side: halo_j(v1, 1, side, 1, ni - 2)
    on_sides(j_side, inner_j, start)
    on_sides(i_side, functools.partial(halo_speed, 0), arrived)
    for h in halves:
        for c in (2 * h, 2 * h + 1):
            on_sides(i_side, lambda side: halo_i(v0, 0, side, c, 1, start_ref), arrived)
        squares0 = planes(v0, 0, 2, ni - 1, (h,), store_v1, squares0)
        on_sides(i_side, lambda side: halo_i(v1, 1, side, 2 * h, 2), start)
    outer_j = [lambda side: halo_j(v1, 2, side, 0, 1), lambda side: halo_j(v1, 3, side, ni - 1, 1)]
    for make in outer_j:
        on_sides(j_side, make, start)

    on_sides(j_side, inner_j, arrived)
    squares1 = planes(v1, 1, ni - 2, 1, halves, store_out, none)
    for make in outer_j:
        on_sides(j_side, make, arrived)
    for h in halves:
        on_sides(i_side, lambda side: halo_i(v1, 1, side, 2 * h, 2), arrived)
        squares1 = planes(v1, 0, 2, ni - 1, (h,), store_out, squares1)

    row = lax.broadcasted_iota(jnp.int32, (8, 128), 0)
    sums = jnp.where(
        row == 0,
        jnp.sum(squares0, axis=0, keepdims=True),
        jnp.where(row == 1, jnp.sum(squares1, axis=0, keepdims=True), 0.0),
    )
    reduction = []
    slot = 0
    for number, stage in enumerate(stages):
        part[number] = sums
        copies = []
        for device in stage:
            copy = pltpu.make_async_remote_copy(
                src_ref=part.at[number], dst_ref=gathered.at[slot], send_sem=r_send.at[slot],
                recv_sem=r_recv.at[slot], device_id=device, device_id_type=MESH,
            )
            copy.start()
            copies.append((slot, copy))
            slot += 1
        for where, copy in copies:
            copy.wait_recv()
            sums = sums + gathered[where]
        reduction += [copy for _, copy in copies]
    root = jnp.sqrt(jnp.sum(sums, axis=1, keepdims=True) / cells_all)
    rms_ref[0] = root[0, 0]
    rms_ref[1] = root[1, 0]

    for copy in reduction:
        copy.wait_send()
    for c in range(chunks):
        on_sides(i_side, lambda side: halo_i(v0, 0, side, c, 1, start_ref), sent)
    for h in halves:
        on_sides(i_side, lambda side: halo_i(v1, 1, side, 2 * h, 2), sent)
    on_sides(j_side, lambda side: halo_j(v0, 0, side, 0, ni), sent)
    for make in [inner_j, *outer_j]:
        on_sides(j_side, make, sent)
    on_sides(i_side, functools.partial(halo_speed, 0), sent)
    on_sides(j_side, functools.partial(halo_speed, 1), sent)


def per_device(adjoint_start, source, flow_state, precond, flux_jac, bc_codes):
    nv, ni, nj, nk = adjoint_start.shape
    cells_all = float(adjoint_start.size * lax.axis_size("stream") * lax.axis_size("span"))
    padded = (ni + 2, nk // 128, nj + 2 * J0, 128)
    hbm = pl.BlockSpec(memory_space=pltpu.HBM)
    in_hbm = functools.partial(pltpu.with_memory_space_constraint, memory_space=pltpu.HBM)
    dma = pltpu.SemaphoreType.DMA
    return pl.pallas_call(
        functools.partial(kernel, cells_all),
        out_shape=(
            pltpu.VMEM(adjoint_start.shape, jnp.float32),
            jax.ShapeDtypeStruct((2,), jnp.float32),
        ),
        in_specs=[hbm, hbm, hbm, hbm, hbm, hbm],
        out_specs=(pl.BlockSpec(memory_space=pltpu.VMEM), pl.BlockSpec(memory_space=pltpu.SMEM)),
        scratch_shapes=[
            pltpu.VMEM((nv, *padded), jnp.float32),
            pltpu.VMEM((nv, *padded), jnp.float32),
            pltpu.VMEM(padded, jnp.float32),
            pltpu.VMEM(flow_state.shape, jnp.float32),
            pltpu.VMEM(source.shape, jnp.float32),
            pltpu.VMEM(precond.shape, jnp.float32),
            pltpu.SMEM((nv, 3, nv), jnp.float32),
            pltpu.VMEM(bc_codes.shape, jnp.int32),
            pltpu.VMEM((ni, nj, 128), jnp.float32),
            pltpu.VMEM((ni, nj, 128), jnp.float32),
            pltpu.VMEM((2, 8, 128), jnp.float32),
            pltpu.VMEM((30, 8, 128), jnp.float32),
            dma((16,)),
            dma((2, 2, nk // 128)),
            dma((2, 2, nk // 128)),
            dma((4, 2)),
            dma((4, 2)),
            dma((2, 2)),
            dma((2, 2)),
            dma((30,)),
            dma((30,)),
        ],
        compiler_params=pltpu.CompilerParams(
            collective_id=0, has_side_effects=True, vmem_limit_bytes=40 * 1024 * 1024
        ),
        cost_estimate=pl.CostEstimate(flops=40_000_000, bytes_accessed=13_000_000, transcendentals=131072),
        name="jacobi_sweeps",
    )(*map(in_hbm, (adjoint_start, source, flow_state, precond, jnp.transpose(flux_jac, (1, 0, 2)), bc_codes)))


def solution(mesh):
    split = P(None, "stream", "span", None)
    return jax.shard_map(
        per_device,
        mesh=mesh,
        in_specs=(split, split, split, P(None, None, "stream", "span", None), P(), P("stream", "span")),
        out_specs=(split, P()),
        check_vma=False,
    )
```

```python
import functools

import jax
import jax.numpy as jnp
from jax import lax
from jax.experimental import pallas as pl
from jax.experimental.pallas import tpu as pltpu
from jax.sharding import PartitionSpec as P

MESH = pl.DeviceIdType.MESH
NV = 5
J0 = 8


def ring(value, step, size):
    return lax.rem(value + step, size)


def reduction_partners(stream, span):
    y, z_lo, x = stream // 8, lax.rem(stream // 4, 2), lax.rem(stream, 4)
    z_hi, core = span // 2, lax.rem(span, 2)

    def at(dy, dl, dx, dh, dc):
        line = ring(y, dy, 4) * 8 + ring(z_lo, dl, 2) * 4 + ring(x, dx, 4)
        return (line, ring(z_hi, dh, 4) * 2 + ring(core, dc, 2))

    far = (2, 1, 3, 0)
    first = [(0, dl, 0, dh, dc) for dh in far for dl in (1, 0) for dc in (1, 0)]
    order = sorted(((dy, dx) for dy in range(4) for dx in range(4)), key=lambda d: -sum(min(t, 4 - t) for t in d))
    second = [(dy, 0, dx, 0, 0) for dy, dx in order]
    return [[at(*step) for step in steps if any(step)] for steps in (first, second)]


def kernel(
    start_ref, source_ref, flow_ref, precond_ref, jac_ref, codes_ref, out, sums_ref,
    v0, v1, speed, flow, source, precond, jac, codes, ghost, flip, part, gathered,
    load_sem, i_send, i_recv, j_send, j_recv, s_send, s_recv, r_send, r_recv,
):
    stream, span = lax.axis_index("stream"), lax.axis_index("span")
    streams, spans = lax.axis_size("stream"), lax.axis_size("span")
    ni, nj, nk = flow.shape[1:]
    chunks = nk // 128
    rows = pl.ds(J0, nj)

    i_side = [(stream > 0, (stream - 1, span)), (stream < streams - 1, (stream + 1, span))]
    j_side = [(span > 0, (stream, span - 1)), (span < spans - 1, (stream, span + 1))]
    stages = reduction_partners(stream, span)

    barrier = pltpu.get_barrier_semaphore()
    for there, device in i_side + j_side:

        @pl.when(there)
        def _():
            pl.semaphore_signal(barrier, inc=1, device_id=device, device_id_type=MESH)

    for device in stages[0] + stages[1]:
        pl.semaphore_signal(barrier, inc=1, device_id=device, device_id_type=MESH)

    load_flow = pltpu.make_async_copy(flow_ref, flow, load_sem.at[0])
    load_start = [
        pltpu.make_async_copy(
            start_ref.at[:, :, :, pl.ds(128 * c, 128)], v0.at[:, pl.ds(1, ni), c, rows, :], load_sem.at[1 + c]
        )
        for c in range(chunks)
    ]
    load_source = pltpu.make_async_copy(source_ref, source, load_sem.at[1 + chunks])
    load_precond = [
        pltpu.make_async_copy(precond_ref.at[u], precond.at[u], load_sem.at[2 + chunks + u]) for u in range(NV)
    ]
    load_jac = pltpu.make_async_copy(jac_ref, jac, load_sem.at[2 + chunks + NV])
    load_codes = pltpu.make_async_copy(codes_ref, codes, load_sem.at[3 + chunks + NV])
    for copy in [load_codes, load_jac, load_flow, *load_start, load_source, *load_precond]:
        copy.start()

    def halo_i(buffer, sweep, side, first, count, source_of=None):
        own, other = (1, ni + 1) if side == 0 else (ni, 0)
        if source_of is None:
            lead = slice(None), own, pl.ds(first, count), rows, slice(None)
            src = buffer.at[lead]
            dst = buffer.at[:, other, pl.ds(first, count), rows, :]
        else:
            src = source_of.at[:, own - 1, :, pl.ds(128 * first, 128)]
            dst = buffer.at[:, other, first, rows, :]
        return pltpu.make_async_remote_copy(
            src_ref=src, dst_ref=dst, send_sem=i_send.at[sweep, side, first],
            recv_sem=i_recv.at[sweep, 1 - side, first], device_id=i_side[side][1], device_id_type=MESH,
        )

    def halo_j(buffer, piece, side, first, count):
        own, other = (J0, J0 + nj) if side == 0 else (J0 + nj - 1, J0 - 1)
        planes = pl.ds(1 + first, count)
        return pltpu.make_async_remote_copy(
            src_ref=buffer.at[:, planes, :, pl.ds(own, 1), :], dst_ref=buffer.at[:, planes, :, pl.ds(other, 1), :],
            send_sem=j_send.at[piece, side], recv_sem=j_recv.at[piece, 1 - side],
            device_id=j_side[side][1], device_id_type=MESH,
        )

    def halo_speed(axis, side):
        if axis == 0:
            own, other = (1, ni + 1) if side == 0 else (ni, 0)
            src, dst = speed.at[own, :, rows, :], speed.at[other, :, rows, :]
            device = i_side[side][1]
        else:
            own, other = (J0, J0 + nj) if side == 0 else (J0 + nj - 1, J0 - 1)
            planes = pl.ds(1, ni)
            src, dst = speed.at[planes, :, pl.ds(own, 1), :], speed.at[planes, :, pl.ds(other, 1), :]
            device = j_side[side][1]
        return pltpu.make_async_remote_copy(
            src_ref=src, dst_ref=dst, send_sem=s_send.at[axis, side], recv_sem=s_recv.at[axis, 1 - side],
            device_id=device, device_id_type=MESH,
        )

    def on_sides(sides, make, act):
        for side in (0, 1):

            @pl.when(sides[side][0])
            def _():
                act(make, side)

    def start(make, side):
        make(side).start()

    def arrived(make, side):
        make(1 - side).wait_recv()

    def sent(make, side):
        make(side).wait_send()

    zero_plane = jnp.zeros((chunks, nj, 128), jnp.float32)
    zero_rows = jnp.zeros((1, 128), jnp.float32)
    for side in (0, 1):
        plane, row = (0, J0 - 1) if side == 0 else (ni + 1, J0 + nj)

        @pl.when(jnp.logical_not(i_side[side][0]))
        def _():
            speed[plane, :, rows, :] = zero_plane
            for u in range(NV):
                v0[u, plane, :, rows, :] = zero_plane
                v1[u, plane, :, rows, :] = zero_plane

        @pl.when(jnp.logical_not(j_side[side][0]))
        def _():
            def clear(i, carry):
                for c in range(chunks):
                    speed[i + 1, c, pl.ds(row, 1), :] = zero_rows
                    for u in range(NV):
                        v0[u, i + 1, c, pl.ds(row, 1), :] = zero_rows
                        v1[u, i + 1, c, pl.ds(row, 1), :] = zero_rows
                return carry

            lax.fori_loop(0, ni, clear, 0)

    lane = lax.broadcasted_iota(jnp.int32, (nj, 128), 1)
    diagonal = lax.broadcasted_iota(jnp.int32, (nj, nj), 0) == lax.broadcasted_iota(jnp.int32, (nj, nj), 1)
    load_codes.wait()
    for i in range(ni):
        line = jnp.broadcast_to(codes[i : i + 1, :].astype(jnp.float32), (nj, nj))
        column = jnp.sum(jnp.where(diagonal, line, 0.0), axis=1, keepdims=True)
        column = jnp.broadcast_to(column, (nj, 128))
        ghost[i] = jnp.where(column == 1.0, 0.0, -1.0)
        flip[i] = jnp.where((column == 0.0) & (lane == 0), 2.0, 0.0)

    load_flow.wait()

    def speeds(i):
        density = flow[0, i]
        momentum = flow[1, i] * flow[1, i] + flow[2, i] * flow[2, i] + flow[3, i] * flow[3, i]
        quarter = 0.25 * (jnp.sqrt(momentum) / density + jnp.sqrt(1.4 * flow[4, i] / density))
        for c in range(chunks):
            speed[i + 1, c, rows, :] = quarter[:, 128 * c : 128 * c + 128]

    def loop_speeds(first, count, stride):
        def step(t, carry):
            speeds(first + stride * t)
            return carry

        lax.fori_loop(0, count, step, 0)

    loop_speeds(0, ni, 1)
    for copy in load_start:
        copy.wait()

    peers = sum(len(stage) for stage in stages)
    for there, _ in i_side + j_side:
        peers = peers + jnp.where(there, 1, 0)
    pl.semaphore_wait(barrier, peers)

    on_sides(j_side, lambda side: halo_j(v0, 0, side, 0, ni), start)
    on_sides(j_side, functools.partial(halo_speed, 1), start)
    on_sides(i_side, functools.partial(halo_speed, 0), start)
    for c in range(chunks):
        on_sides(i_side, lambda side: halo_i(v0, 0, side, c, 1, start_ref), start)

    load_jac.wait()
    half = [[[0.5 * jac[u, d, v] for v in range(NV)] for u in range(NV)] for d in range(3)]

    def along_k(read, h, mirror):
        own = [read(2 * h), read(2 * h + 1)]
        up = [pltpu.roll(x, 1, 1) for x in own]
        down = [pltpu.roll(x, 127, 1) for x in own]
        before = mirror * own[0] if h == 0 else pltpu.roll(read(2 * h - 1), 1, 1)
        after = jnp.zeros_like(own[0]) if 2 * h + 2 == chunks else pltpu.roll(read(2 * h + 2), 127, 1)
        first, last = lane == 0, lane == 127
        left = [jnp.where(first, before, up[0]), jnp.where(first, up[0], up[1])]
        right = [jnp.where(last, down[1], down[0]), jnp.where(last, after, down[1])]
        return own, left, right

    def update(v, i, h, store):
        mirror = ghost[i]
        s_own, s_left, s_right = along_k(lambda c: speed[i + 1, c, rows, :], h, mirror)
        around = [along_k(lambda c, u=u: v[u, i + 1, c, rows, :], h, mirror) for u in range(NV)]
        squares = jnp.zeros((nj, 128), jnp.float32)
        for q in (0, 1):
            c = 2 * h + q
            own = [around[u][0][q] for u in range(NV)]
            s = s_own[q]
            places = [
                (speed[i, c, rows, :], lambda u, c=c: v[u, i, c, rows, :]),
                (speed[i + 2, c, rows, :], lambda u, c=c: v[u, i + 2, c, rows, :]),
                (speed[i + 1, c, pl.ds(J0 - 1, nj), :], lambda u, c=c: v[u, i + 1, c, pl.ds(J0 - 1, nj), :]),
                (speed[i + 1, c, pl.ds(J0 + 1, nj), :], lambda u, c=c: v[u, i + 1, c, pl.ds(J0 + 1, nj), :]),
                (s_left[q], lambda u, q=q: around[u][1][q]),
                (s_right[q], lambda u, q=q: around[u][2][q]),
            ]
            weights = [s + beside for beside, _ in places]
            total = functools.reduce(jnp.add, weights)
            r = [source[u, i, :, 128 * c : 128 * c + 128] - total * own[u] for u in range(NV)]
            for d in range(3):
                jump = []
                for u in range(NV):
                    low, high = places[2 * d][1](u), places[2 * d + 1][1](u)
                    r[u] = r[u] + (weights[2 * d] * low + weights[2 * d + 1] * high)
                    jump.append(high - low)
                for w in range(NV):
                    for u in range(NV):
                        r[w] = r[w] + half[d][u][w] * jump[u]
            if c == 0:
                wall = s * own[3]
                for u in range(NV):
                    wall = wall + half[2][u][3] * own[u]
                r[3] = r[3] - flip[i] * wall
            for w in range(NV):
                new = own[w]
                for u in range(NV):
                    new = new + precond[u, w, i, :, 128 * c : 128 * c + 128] * r[u]
                store(w, c, new)
                squares = squares + r[w] * r[w]
        return squares

    def planes(v, first, count, stride, halves, store, squares):
        def step(t, carry):
            i = first + stride * t
            for h in halves:
                carry = carry + update(v, i, h, functools.partial(store, i))
            return carry

        return lax.fori_loop(0, count, step, squares)

    def store_v1(i, w, c, new):
        v1[w, i + 1, c, rows, :] = new

    def store_out(i, w, c, new):
        out[w, i, :, 128 * c : 128 * c + 128] = new

    load_source.wait()
    for copy in load_precond:
        copy.wait()

    none = jnp.zeros((nj, 128), jnp.float32)
    halves = tuple(range(chunks // 2))

    on_sides(j_side, functools.partial(halo_speed, 1), arrived)
    on_sides(j_side, lambda side: halo_j(v0, 0, side, 0, ni), arrived)
    squares0 = planes(v0, 1, ni - 2, 1, halves, store_v1, none)
    inner_j = lambda side: halo_j(v1, 1, side, 1, ni - 2)
    on_sides(j_side, inner_j, start)
    on_sides(i_side, functools.partial(halo_speed, 0), arrived)
    for h in halves:
        for c in (2 * h, 2 * h + 1):
            on_sides(i_side, lambda side: halo_i(v0, 0, side, c, 1, start_ref), arrived)
        squares0 = planes(v0, 0, 2, ni - 1, (h,), store_v1, squares0)
        on_sides(i_side, lambda side: halo_i(v1, 1, side, 2 * h, 2), start)
    outer_j = [lambda side: halo_j(v1, 2, side, 0, 1), lambda side: halo_j(v1, 3, side, ni - 1, 1)]
    for make in outer_j:
        on_sides(j_side, make, start)

    on_sides(j_side, inner_j, arrived)
    squares1 = planes(v1, 1, ni - 2, 1, halves, store_out, none)
    for make in outer_j:
        on_sides(j_side, make, arrived)
    for h in halves:
        on_sides(i_side, lambda side: halo_i(v1, 1, side, 2 * h, 2), arrived)
        squares1 = planes(v1, 0, 2, ni - 1, (h,), store_out, squares1)

    row = lax.broadcasted_iota(jnp.int32, (8, 128), 0)
    sums = jnp.where(
        row == 0,
        jnp.sum(squares0, axis=0, keepdims=True),
        jnp.where(row == 1, jnp.sum(squares1, axis=0, keepdims=True), 0.0),
    )
    reduction = []
    slot = 0
    for number, stage in enumerate(stages):
        part[number] = sums
        copies = []
        for device in stage:
            copy = pltpu.make_async_remote_copy(
                src_ref=part.at[number], dst_ref=gathered.at[slot], send_sem=r_send.at[slot],
                recv_sem=r_recv.at[slot], device_id=device, device_id_type=MESH,
            )
            copy.start()
            copies.append((slot, copy))
            slot += 1
        for where, copy in copies:
            copy.wait_recv()
            sums = sums + gathered[where]
        reduction += [copy for _, copy in copies]
    sums_ref[...] = sums

    for copy in reduction:
        copy.wait_send()
    for c in range(chunks):
        on_sides(i_side, lambda side: halo_i(v0, 0, side, c, 1, start_ref), sent)
    for h in halves:
        on_sides(i_side, lambda side: halo_i(v1, 1, side, 2 * h, 2), sent)
    on_sides(j_side, lambda side: halo_j(v0, 0, side, 0, ni), sent)
    for make in [inner_j, *outer_j]:
        on_sides(j_side, make, sent)
    on_sides(i_side, functools.partial(halo_speed, 0), sent)
    on_sides(j_side, functools.partial(halo_speed, 1), sent)


def deliver(cells_all, adjoint_vmem, sums_ref, adjoint_ref, rms_ref, sem):
    copy = pltpu.make_async_copy(adjoint_vmem, adjoint_ref, sem)
    copy.start()
    root = jnp.sqrt(jnp.sum(sums_ref[...], axis=1, keepdims=True) / cells_all)
    rms_ref[0] = root[0, 0]
    rms_ref[1] = root[1, 0]
    copy.wait()


def per_device(adjoint_start, source, flow_state, precond, flux_jac, bc_codes):
    nv, ni, nj, nk = adjoint_start.shape
    cells_all = float(adjoint_start.size * lax.axis_size("stream") * lax.axis_size("span"))
    padded = (ni + 2, nk // 128, nj + 2 * J0, 128)
    hbm, vmem = pl.BlockSpec(memory_space=pltpu.HBM), pl.BlockSpec(memory_space=pltpu.VMEM)
    in_hbm = functools.partial(pltpu.with_memory_space_constraint, memory_space=pltpu.HBM)
    dma = pltpu.SemaphoreType.DMA
    adjoint, sums = pl.pallas_call(
        kernel,
        out_shape=(
            pltpu.VMEM(adjoint_start.shape, jnp.float32),
            pltpu.VMEM((8, 128), jnp.float32),
        ),
        in_specs=[hbm, hbm, hbm, hbm, hbm, hbm],
        out_specs=(vmem, vmem),
        scratch_shapes=[
            pltpu.VMEM((nv, *padded), jnp.float32),
            pltpu.VMEM((nv, *padded), jnp.float32),
            pltpu.VMEM(padded, jnp.float32),
            pltpu.VMEM(flow_state.shape, jnp.float32),
            pltpu.VMEM(source.shape, jnp.float32),
            pltpu.VMEM(precond.shape, jnp.float32),
            pltpu.SMEM((nv, 3, nv), jnp.float32),
            pltpu.VMEM(bc_codes.shape, jnp.int32),
            pltpu.VMEM((ni, nj, 128), jnp.float32),
            pltpu.VMEM((ni, nj, 128), jnp.float32),
            pltpu.VMEM((2, 8, 128), jnp.float32),
            pltpu.VMEM((30, 8, 128), jnp.float32),
            dma((16,)),
            dma((2, 2, nk // 128)),
            dma((2, 2, nk // 128)),
            dma((4, 2)),
            dma((4, 2)),
            dma((2, 2)),
            dma((2, 2)),
            dma((30,)),
            dma((30,)),
        ],
        compiler_params=pltpu.CompilerParams(
            collective_id=0, has_side_effects=True, vmem_limit_bytes=40 * 1024 * 1024
        ),
        cost_estimate=pl.CostEstimate(flops=40_000_000, bytes_accessed=13_000_000, transcendentals=131072),
        name="jacobi_sweeps",
    )(*map(in_hbm, (adjoint_start, source, flow_state, precond, jnp.transpose(flux_jac, (1, 0, 2)), bc_codes)))
    return pl.pallas_call(
        functools.partial(deliver, cells_all),
        out_shape=(
            jax.ShapeDtypeStruct(adjoint.shape, jnp.float32),
            jax.ShapeDtypeStruct((2,), jnp.float32),
        ),
        in_specs=[vmem, vmem],
        out_specs=(hbm, pl.BlockSpec(memory_space=pltpu.SMEM)),
        scratch_shapes=[dma],
        compiler_params=pltpu.CompilerParams(vmem_limit_bytes=4 * 1024 * 1024),
        name="deliver",
    )(*(pltpu.with_memory_space_constraint(x, memory_space=pltpu.VMEM) for x in (adjoint, sums)))


def solution(mesh):
    split = P(None, "stream", "span", None)
    return jax.shard_map(
        per_device,
        mesh=mesh,
        in_specs=(split, split, split, P(None, None, "stream", "span", None), P(), P("stream", "span")),
        out_specs=(split, P()),
        check_vma=False,
    )
```

```python
import functools

import jax
import jax.numpy as jnp
from jax import lax
from jax.experimental import pallas as pl
from jax.experimental.pallas import tpu as pltpu
from jax.sharding import PartitionSpec as P

MESH = pl.DeviceIdType.MESH
NV = 5
J0 = 8


def ring(value, step, size):
    return lax.rem(value + step, size)


def reduction_partners(stream, span):
    y, z_lo, x = stream // 8, lax.rem(stream // 4, 2), lax.rem(stream, 4)
    z_hi, core = span // 2, lax.rem(span, 2)

    def at(dy, dl, dx, dh, dc):
        line = ring(y, dy, 4) * 8 + ring(z_lo, dl, 2) * 4 + ring(x, dx, 4)
        return (line, ring(z_hi, dh, 4) * 2 + ring(core, dc, 2))

    far = (2, 1, 3, 0)
    first = [(0, dl, 0, dh, dc) for dh in far for dl in (1, 0) for dc in (1, 0)]
    order = sorted(((dy, dx) for dy in range(4) for dx in range(4)), key=lambda d: -sum(min(t, 4 - t) for t in d))
    second = [(dy, 0, dx, 0, 0) for dy, dx in order]
    return [[at(*step) for step in steps if any(step)] for steps in (first, second)]


def kernel(
    start_ref, source_ref, flow_ref, precond_ref, jac_ref, codes_ref, out, sums_ref,
    v0, v1, speed, i_in, j_in, s_i_in, s_j_in, residual, flow, source, precond, jac, codes, ghost, flip, part, gathered,
    load_sem, i_send, i_recv, j_send, j_recv, s_send, s_recv, r_send, r_recv,
):
    stream, span = lax.axis_index("stream"), lax.axis_index("span")
    streams, spans = lax.axis_size("stream"), lax.axis_size("span")
    ni, nj, nk = flow.shape[1:]
    chunks = nk // 128
    rows = pl.ds(J0, nj)

    i_side = [(stream > 0, (stream - 1, span)), (stream < streams - 1, (stream + 1, span))]
    j_side = [(span > 0, (stream, span - 1)), (span < spans - 1, (stream, span + 1))]
    stages = reduction_partners(stream, span)

    barrier = pltpu.get_barrier_semaphore()
    for there, device in i_side + j_side:

        @pl.when(there)
        def _():
            pl.semaphore_signal(barrier, inc=1, device_id=device, device_id_type=MESH)

    for device in stages[0] + stages[1]:
        pl.semaphore_signal(barrier, inc=1, device_id=device, device_id_type=MESH)

    load_flow = pltpu.make_async_copy(flow_ref, flow, load_sem.at[0])
    load_start = [
        pltpu.make_async_copy(
            start_ref.at[:, :, :, pl.ds(128 * c, 128)], v0.at[:, pl.ds(1, ni), c, rows, :], load_sem.at[1 + c]
        )
        for c in range(chunks)
    ]
    load_source = pltpu.make_async_copy(source_ref, source, load_sem.at[1 + chunks])
    load_precond = [
        pltpu.make_async_copy(precond_ref.at[u], precond.at[u], load_sem.at[2 + chunks + u]) for u in range(NV)
    ]
    load_jac = pltpu.make_async_copy(jac_ref, jac, load_sem.at[2 + chunks + NV])
    load_codes = pltpu.make_async_copy(codes_ref, codes, load_sem.at[3 + chunks + NV])
    for copy in [load_codes, load_jac, load_flow, *load_start, load_source, *load_precond]:
        copy.start()

    def remote(src, dst, send_sem, recv_sem, device):
        return pltpu.make_async_remote_copy(
            src_ref=src, dst_ref=dst, send_sem=send_sem, recv_sem=recv_sem, device_id=device, device_id_type=MESH
        )

    def halo_i(sweep, side, first, count):
        own = 0 if side == 0 else ni - 1
        if sweep == 0:
            src = start_ref.at[:, own, :, pl.ds(128 * first, 128)]
            dst = i_in.at[0, 1 - side, :, first]
        else:
            src = v1.at[:, own + 1, pl.ds(first, count), rows, :]
            dst = i_in.at[1, 1 - side, :, pl.ds(first, count)]
        return remote(src, dst, i_send.at[sweep, side, first], i_recv.at[sweep, 1 - side, first], i_side[side][1])

    def halo_j(sweep, piece, side, first, count):
        own, other = (0, nj - 1) if side == 0 else (nj - 1, 0)
        src = (v0, v1)[sweep].at[:, pl.ds(1 + first, count), :, pl.ds(J0 + own, 1), :]
        dst = j_in.at[sweep, :, pl.ds(first, count), :, pl.ds(other, 1), :]
        return remote(src, dst, j_send.at[piece, side], j_recv.at[piece, 1 - side], j_side[side][1])

    def halo_speed(axis, side):
        if axis == 0:
            src, dst = speed.at[1 if side == 0 else ni, :, rows, :], s_i_in.at[1 - side]
            device = i_side[side][1]
        else:
            own, other = (0, nj - 1) if side == 0 else (nj - 1, 0)
            src, dst = speed.at[pl.ds(1, ni), :, pl.ds(J0 + own, 1), :], s_j_in.at[:, :, pl.ds(other, 1), :]
            device = j_side[side][1]
        return remote(src, dst, s_send.at[axis, side], s_recv.at[axis, 1 - side], device)

    def on_sides(sides, make, act):
        for side in (0, 1):

            @pl.when(sides[side][0])
            def _():
                act(make, side)

    def start(make, side):
        make(side).start()

    def arrived(make, side):
        make(1 - side).wait_recv()

    def sent(make, side):
        make(side).wait_send()

    zero_plane = jnp.zeros((chunks, nj, 128), jnp.float32)
    zero_row = jnp.zeros((1, 128), jnp.float32)
    for plane in (0, ni + 1):
        speed[plane, :, rows, :] = zero_plane
        for u in range(NV):
            v0[u, plane, :, rows, :] = zero_plane
            v1[u, plane, :, rows, :] = zero_plane

    def clear_beside(i, carry):
        for c in range(chunks):
            for row in (J0 - 1, J0 + nj):
                speed[i + 1, c, pl.ds(row, 1), :] = zero_row
                for u in range(NV):
                    v0[u, i + 1, c, pl.ds(row, 1), :] = zero_row
                    v1[u, i + 1, c, pl.ds(row, 1), :] = zero_row
        return carry

    lax.fori_loop(0, ni, clear_beside, 0)
    for side in (0, 1):

        @pl.when(jnp.logical_not(i_side[side][0]))
        def _():
            s_i_in[side] = zero_plane
            for u in range(NV):
                i_in[0, side, u] = zero_plane
                i_in[1, side, u] = zero_plane

        @pl.when(jnp.logical_not(j_side[side][0]))
        def _():
            row = 0 if side == 0 else nj - 1

            def clear(i, carry):
                for c in range(chunks):
                    s_j_in[i, c, pl.ds(row, 1), :] = zero_row
                    for u in range(NV):
                        j_in[0, u, i, c, pl.ds(row, 1), :] = zero_row
                        j_in[1, u, i, c, pl.ds(row, 1), :] = zero_row
                return carry

            lax.fori_loop(0, ni, clear, 0)

    lane = lax.broadcasted_iota(jnp.int32, (nj, 128), 1)
    diagonal = lax.broadcasted_iota(jnp.int32, (nj, nj), 0) == lax.broadcasted_iota(jnp.int32, (nj, nj), 1)
    load_codes.wait()
    for i in range(ni):
        line = jnp.broadcast_to(codes[i : i + 1, :].astype(jnp.float32), (nj, nj))
        column = jnp.sum(jnp.where(diagonal, line, 0.0), axis=1, keepdims=True)
        column = jnp.broadcast_to(column, (nj, 128))
        ghost[i] = jnp.where(column == 1.0, 0.0, -1.0)
        flip[i] = jnp.where((column == 0.0) & (lane == 0), 2.0, 0.0)

    load_flow.wait()

    def speeds(i):
        density = flow[0, i]
        momentum = flow[1, i] * flow[1, i] + flow[2, i] * flow[2, i] + flow[3, i] * flow[3, i]
        quarter = 0.25 * (jnp.sqrt(momentum) / density + jnp.sqrt(1.4 * flow[4, i] / density))
        for c in range(chunks):
            speed[i + 1, c, rows, :] = quarter[:, 128 * c : 128 * c + 128]

    def loop_speeds(first, count, stride):
        def step(t, carry):
            speeds(first + stride * t)
            return carry

        lax.fori_loop(0, count, step, 0)

    loop_speeds(0, ni, 1)
    for copy in load_start:
        copy.wait()

    peers = sum(len(stage) for stage in stages)
    for there, _ in i_side + j_side:
        peers = peers + jnp.where(there, 1, 0)
    pl.semaphore_wait(barrier, peers)

    on_sides(j_side, lambda side: halo_j(0, 0, side, 0, ni), start)
    on_sides(j_side, functools.partial(halo_speed, 1), start)
    on_sides(i_side, functools.partial(halo_speed, 0), start)
    for c in range(chunks):
        on_sides(i_side, lambda side: halo_i(0, side, c, 1), start)

    load_jac.wait()
    half = [[[0.5 * jac[u, d, v] for v in range(NV)] for u in range(NV)] for d in range(3)]

    def along_k(read, h, mirror):
        own = [read(2 * h), read(2 * h + 1)]
        up = [pltpu.roll(x, 1, 1) for x in own]
        down = [pltpu.roll(x, 127, 1) for x in own]
        before = mirror * own[0] if h == 0 else pltpu.roll(read(2 * h - 1), 1, 1)
        after = jnp.zeros_like(own[0]) if 2 * h + 2 == chunks else pltpu.roll(read(2 * h + 2), 127, 1)
        first, last = lane == 0, lane == 127
        left = [jnp.where(first, before, up[0]), jnp.where(first, up[0], up[1])]
        right = [jnp.where(last, down[1], down[0]), jnp.where(last, after, down[1])]
        return own, left, right

    def inside(v, i, h):
        mirror = ghost[i]
        s_own, s_left, s_right = along_k(lambda c: speed[i + 1, c, rows, :], h, mirror)
        around = [along_k(lambda c, u=u: v[u, i + 1, c, rows, :], h, mirror) for u in range(NV)]
        for q in (0, 1):
            c = 2 * h + q
            own = [around[u][0][q] for u in range(NV)]
            s = s_own[q]
            places = [
                (speed[i, c, rows, :], lambda u, c=c: v[u, i, c, rows, :]),
                (speed[i + 2, c, rows, :], lambda u, c=c: v[u, i + 2, c, rows, :]),
                (speed[i + 1, c, pl.ds(J0 - 1, nj), :], lambda u, c=c: v[u, i + 1, c, pl.ds(J0 - 1, nj), :]),
                (speed[i + 1, c, pl.ds(J0 + 1, nj), :], lambda u, c=c: v[u, i + 1, c, pl.ds(J0 + 1, nj), :]),
                (s_left[q], lambda u, q=q: around[u][1][q]),
                (s_right[q], lambda u, q=q: around[u][2][q]),
            ]
            weights = [s + beside for beside, _ in places]
            total = functools.reduce(jnp.add, weights)
            r = [source[u, i, :, 128 * c : 128 * c + 128] - total * own[u] for u in range(NV)]
            for d in range(3):
                jump = []
                for u in range(NV):
                    low, high = places[2 * d][1](u), places[2 * d + 1][1](u)
                    r[u] = r[u] + (weights[2 * d] * low + weights[2 * d + 1] * high)
                    jump.append(high - low)
                for w in range(NV):
                    for u in range(NV):
                        r[w] = r[w] + half[d][u][w] * jump[u]
            if c == 0:
                wall = s * own[3]
                for u in range(NV):
                    wall = wall + half[2][u][3] * own[u]
                r[3] = r[3] - flip[i] * wall
            for u in range(NV):
                residual[u, i, c] = r[u]

    row = lax.broadcasted_iota(jnp.int32, (nj, 128), 0)
    edge = (row == 0) | (row == nj - 1)
    edge_sign = jnp.where(row < nj // 2, -1.0, 1.0)

    def add_beside(r, s, own, s_beside, beside, d, sign):
        weight = s + s_beside
        signed = [sign * x for x in beside]
        for w in range(NV):
            r[w] = r[w] + (weight * beside[w] - s_beside * own[w])
            for u in range(NV):
                r[w] = r[w] + half[d][u][w] * signed[u]

    def whole(v, sweep, i, c, side):
        r = [residual[u, i, c] for u in range(NV)]
        s = speed[i + 1, c, rows, :]
        own = [v[u, i + 1, c, rows, :] for u in range(NV)]
        beside = [jnp.where(edge, j_in[sweep, u, i, c], 0.0) for u in range(NV)]
        add_beside(r, s, own, jnp.where(edge, s_j_in[i, c], 0.0), beside, 1, edge_sign)
        if side is not None:
            beside = [i_in[sweep, side, u, c] for u in range(NV)]
            add_beside(r, s, own, s_i_in[side, c], beside, 0, (2 * side - 1).astype(jnp.float32))
        return r, own

    def preconditioned(r, own, i, c):
        new = []
        for w in range(NV):
            total = own[w]
            for u in range(NV):
                total = total + precond[u, w, i, :, 128 * c : 128 * c + 128] * r[u]
            new.append(total)
        return new

    def first_sweep(i, c, side, squares):
        r, own = whole(v0, 0, i, c, side)
        for w, new in enumerate(preconditioned(r, own, i, c)):
            v1[w, i + 1, c, rows, :] = new
        return squares + functools.reduce(jnp.add, [x * x for x in r])

    def second_sweep(i, c, side, squares):
        r, _ = whole(v1, 1, i, c, side)
        for u in range(NV):
            residual[u, i, c] = r[u]
        return squares + functools.reduce(jnp.add, [x * x for x in r])

    def all_inside(v):
        def step(i, carry):
            for h in halves:
                inside(v, i, h)
            return carry

        lax.fori_loop(0, ni, step, 0)

    def inner_planes(act, squares):
        def step(i, carry):
            for c in range(chunks):
                carry = act(i, c, None, carry)
            return carry

        return lax.fori_loop(1, ni - 1, step, squares)

    def outer_planes(act, h, squares):
        def step(side, carry):
            for c in (2 * h, 2 * h + 1):
                carry = act((ni - 1) * side, c, side, carry)
            return carry

        return lax.fori_loop(0, 2, step, squares)

    none = jnp.zeros((nj, 128), jnp.float32)
    halves = tuple(range(chunks // 2))

    load_source.wait()
    all_inside(v0)
    for copy in load_precond:
        copy.wait()
    on_sides(j_side, functools.partial(halo_speed, 1), arrived)
    on_sides(j_side, lambda side: halo_j(0, 0, side, 0, ni), arrived)
    squares0 = inner_planes(first_sweep, none)
    inner_j = lambda side: halo_j(1, 1, side, 1, ni - 2)
    on_sides(j_side, inner_j, start)
    on_sides(i_side, functools.partial(halo_speed, 0), arrived)
    for h in halves:
        for c in (2 * h, 2 * h + 1):
            on_sides(i_side, lambda side: halo_i(0, side, c, 1), arrived)
        squares0 = outer_planes(first_sweep, h, squares0)
        on_sides(i_side, lambda side: halo_i(1, side, 2 * h, 2), start)
    outer_j = [lambda side: halo_j(1, 2, side, 0, 1), lambda side: halo_j(1, 3, side, ni - 1, 1)]
    for make in outer_j:
        on_sides(j_side, make, start)

    all_inside(v1)
    on_sides(j_side, inner_j, arrived)
    squares1 = inner_planes(second_sweep, none)
    for make in outer_j:
        on_sides(j_side, make, arrived)
    for h in halves:
        on_sides(i_side, lambda side: halo_i(1, side, 2 * h, 2), arrived)
        squares1 = outer_planes(second_sweep, h, squares1)

    def last(i, carry):
        for c in range(chunks):
            r = [residual[u, i, c] for u in range(NV)]
            own = [v1[u, i + 1, c, rows, :] for u in range(NV)]
            for w, new in enumerate(preconditioned(r, own, i, c)):
                out[w, i, :, 128 * c : 128 * c + 128] = new
        return carry

    line = lax.broadcasted_iota(jnp.int32, (8, 128), 0)
    sums = jnp.where(
        line == 0,
        jnp.sum(squares0, axis=0, keepdims=True),
        jnp.where(line == 1, jnp.sum(squares1, axis=0, keepdims=True), 0.0),
    )
    reduction = []
    slot = 0
    for number, stage in enumerate(stages):
        part[number] = sums
        copies = []
        for device in stage:
            copy = pltpu.make_async_remote_copy(
                src_ref=part.at[number], dst_ref=gathered.at[slot], send_sem=r_send.at[slot],
                recv_sem=r_recv.at[slot], device_id=device, device_id_type=MESH,
            )
            copy.start()
            copies.append((slot, copy))
            slot += 1
        if number == 0:
            lax.fori_loop(0, ni, last, 0)
        for where, copy in copies:
            copy.wait_recv()
            sums = sums + gathered[where]
        reduction += [copy for _, copy in copies]
    sums_ref[...] = sums

    for copy in reduction:
        copy.wait_send()
    for c in range(chunks):
        on_sides(i_side, lambda side: halo_i(0, side, c, 1), sent)
    for h in halves:
        on_sides(i_side, lambda side: halo_i(1, side, 2 * h, 2), sent)
    on_sides(j_side, lambda side: halo_j(0, 0, side, 0, ni), sent)
    for make in [inner_j, *outer_j]:
        on_sides(j_side, make, sent)
    on_sides(i_side, functools.partial(halo_speed, 0), sent)
    on_sides(j_side, functools.partial(halo_speed, 1), sent)


def deliver(cells_all, adjoint_vmem, sums_ref, adjoint_ref, rms_ref, sem):
    copy = pltpu.make_async_copy(adjoint_vmem, adjoint_ref, sem)
    copy.start()
    root = jnp.sqrt(jnp.sum(sums_ref[...], axis=1, keepdims=True) / cells_all)
    rms_ref[0] = root[0, 0]
    rms_ref[1] = root[1, 0]
    copy.wait()


def per_device(adjoint_start, source, flow_state, precond, flux_jac, bc_codes):
    nv, ni, nj, nk = adjoint_start.shape
    cells_all = float(adjoint_start.size * lax.axis_size("stream") * lax.axis_size("span"))
    block = (ni, nk // 128, nj, 128)
    padded = (ni + 2, nk // 128, nj + 2 * J0, 128)
    hbm, vmem = pl.BlockSpec(memory_space=pltpu.HBM), pl.BlockSpec(memory_space=pltpu.VMEM)
    in_hbm = functools.partial(pltpu.with_memory_space_constraint, memory_space=pltpu.HBM)
    dma = pltpu.SemaphoreType.DMA
    adjoint, sums = pl.pallas_call(
        kernel,
        out_shape=(
            pltpu.VMEM(adjoint_start.shape, jnp.float32),
            pltpu.VMEM((8, 128), jnp.float32),
        ),
        in_specs=[hbm, hbm, hbm, hbm, hbm, hbm],
        out_specs=(vmem, vmem),
        scratch_shapes=[
            pltpu.VMEM((nv, *padded), jnp.float32),
            pltpu.VMEM((nv, *padded), jnp.float32),
            pltpu.VMEM(padded, jnp.float32),
            pltpu.VMEM((2, 2, nv, nk // 128, nj, 128), jnp.float32),
            pltpu.VMEM((2, nv, *block), jnp.float32),
            pltpu.VMEM((2, nk // 128, nj, 128), jnp.float32),
            pltpu.VMEM(block, jnp.float32),
            pltpu.VMEM((nv, *block), jnp.float32),
            pltpu.VMEM(flow_state.shape, jnp.float32),
            pltpu.VMEM(source.shape, jnp.float32),
            pltpu.VMEM(precond.shape, jnp.float32),
            pltpu.SMEM((nv, 3, nv), jnp.float32),
            pltpu.VMEM(bc_codes.shape, jnp.int32),
            pltpu.VMEM((ni, nj, 128), jnp.float32),
            pltpu.VMEM((ni, nj, 128), jnp.float32),
            pltpu.VMEM((2, 8, 128), jnp.float32),
            pltpu.VMEM((30, 8, 128), jnp.float32),
            dma((16,)),
            dma((2, 2, nk // 128)),
            dma((2, 2, nk // 128)),
            dma((4, 2)),
            dma((4, 2)),
            dma((2, 2)),
            dma((2, 2)),
            dma((30,)),
            dma((30,)),
        ],
        compiler_params=pltpu.CompilerParams(
            collective_id=0, has_side_effects=True, vmem_limit_bytes=40 * 1024 * 1024
        ),
        cost_estimate=pl.CostEstimate(flops=40_000_000, bytes_accessed=13_000_000, transcendentals=131072),
        name="jacobi_sweeps",
    )(*map(in_hbm, (adjoint_start, source, flow_state, precond, jnp.transpose(flux_jac, (1, 0, 2)), bc_codes)))
    return pl.pallas_call(
        functools.partial(deliver, cells_all),
        out_shape=(
            jax.ShapeDtypeStruct(adjoint.shape, jnp.float32),
            jax.ShapeDtypeStruct((2,), jnp.float32),
        ),
        in_specs=[vmem, vmem],
        out_specs=(hbm, pl.BlockSpec(memory_space=pltpu.SMEM)),
        scratch_shapes=[dma],
        compiler_params=pltpu.CompilerParams(vmem_limit_bytes=4 * 1024 * 1024),
        name="deliver",
    )(*(pltpu.with_memory_space_constraint(x, memory_space=pltpu.VMEM) for x in (adjoint, sums)))


def solution(mesh):
    split = P(None, "stream", "span", None)
    return jax.shard_map(
        per_device,
        mesh=mesh,
        in_specs=(split, split, split, P(None, None, "stream", "span", None), P(), P("stream", "span")),
        out_specs=(split, P()),
        check_vma=False,
    )
```

```python
import functools

import jax
import jax.numpy as jnp
from jax import lax
from jax.experimental import pallas as pl
from jax.experimental.pallas import tpu as pltpu
from jax.sharding import PartitionSpec as P

MESH = pl.DeviceIdType.MESH
NV = 5
J0 = 8


def ring(value, step, size):
    return lax.rem(value + step, size)


def reduction_partners(stream, span):
    y, z_lo, x = stream // 8, lax.rem(stream // 4, 2), lax.rem(stream, 4)
    z_hi, core = span // 2, lax.rem(span, 2)

    def at(dy, dl, dx, dh, dc):
        line = ring(y, dy, 4) * 8 + ring(z_lo, dl, 2) * 4 + ring(x, dx, 4)
        return (line, ring(z_hi, dh, 4) * 2 + ring(core, dc, 2))

    far = (2, 1, 3, 0)
    first = [(0, dl, 0, dh, dc) for dh in far for dl in (1, 0) for dc in (1, 0)]
    order = sorted(((dy, dx) for dy in range(4) for dx in range(4)), key=lambda d: -sum(min(t, 4 - t) for t in d))
    second = [(dy, 0, dx, 0, 0) for dy, dx in order]
    return [[at(*step) for step in steps if any(step)] for steps in (first, second)]


def kernel(
    start_ref, source_ref, flow_ref, precond_ref, jac_ref, codes_ref, out, sums_ref,
    v0, v1, speed, i_in, j_in, s_i_in, s_j_in, residual, flow, source, precond, jac, codes, ghost, flip, part, gathered,
    load_sem, i_send, i_recv, j_send, j_recv, s_send, s_recv, r_send, r_recv,
):
    stream, span = lax.axis_index("stream"), lax.axis_index("span")
    streams, spans = lax.axis_size("stream"), lax.axis_size("span")
    ni, nj, nk = flow.shape[1:]
    chunks = nk // 128
    rows = pl.ds(J0, nj)

    i_side = [(stream > 0, (stream - 1, span)), (stream < streams - 1, (stream + 1, span))]
    j_side = [(span > 0, (stream, span - 1)), (span < spans - 1, (stream, span + 1))]
    stages = reduction_partners(stream, span)

    barrier = pltpu.get_barrier_semaphore()
    for there, device in i_side + j_side:

        @pl.when(there)
        def _():
            pl.semaphore_signal(barrier, inc=1, device_id=device, device_id_type=MESH)

    load_flow = pltpu.make_async_copy(flow_ref, flow, load_sem.at[0])
    load_start = [
        pltpu.make_async_copy(
            start_ref.at[:, :, :, pl.ds(128 * c, 128)], v0.at[:, pl.ds(1, ni), c, rows, :], load_sem.at[1 + c]
        )
        for c in range(chunks)
    ]
    load_source = pltpu.make_async_copy(source_ref, source, load_sem.at[1 + chunks])
    load_precond = [
        pltpu.make_async_copy(precond_ref.at[u], precond.at[u], load_sem.at[2 + chunks + u]) for u in range(NV)
    ]
    load_jac = pltpu.make_async_copy(jac_ref, jac, load_sem.at[2 + chunks + NV])
    load_codes = pltpu.make_async_copy(codes_ref, codes, load_sem.at[3 + chunks + NV])
    for copy in [load_flow, *load_start, load_codes, load_jac, load_source, *load_precond]:
        copy.start()

    for device in stages[0] + stages[1]:
        pl.semaphore_signal(barrier, inc=1, device_id=device, device_id_type=MESH)

    def remote(src, dst, send_sem, recv_sem, device):
        return pltpu.make_async_remote_copy(
            src_ref=src, dst_ref=dst, send_sem=send_sem, recv_sem=recv_sem, device_id=device, device_id_type=MESH
        )

    def halo_i(sweep, side, first, count):
        own = 0 if side == 0 else ni - 1
        if sweep == 0:
            src = start_ref.at[:, own, :, pl.ds(128 * first, 128)]
            dst = i_in.at[0, 1 - side, :, first]
        else:
            src = v1.at[:, own + 1, pl.ds(first, count), rows, :]
            dst = i_in.at[1, 1 - side, :, pl.ds(first, count)]
        return remote(src, dst, i_send.at[sweep, side, first], i_recv.at[sweep, 1 - side, first], i_side[side][1])

    def halo_j(sweep, piece, side, first, count):
        own, other = (0, nj - 1) if side == 0 else (nj - 1, 0)
        src = (v0, v1)[sweep].at[:, pl.ds(1 + first, count), :, pl.ds(J0 + own, 1), :]
        dst = j_in.at[sweep, :, pl.ds(first, count), :, pl.ds(other, 1), :]
        return remote(src, dst, j_send.at[piece, side], j_recv.at[piece, 1 - side], j_side[side][1])

    def halo_speed(axis, side):
        if axis == 0:
            src, dst = speed.at[1 if side == 0 else ni, :, rows, :], s_i_in.at[1 - side]
            device = i_side[side][1]
        else:
            own, other = (0, nj - 1) if side == 0 else (nj - 1, 0)
            src, dst = speed.at[pl.ds(1, ni), :, pl.ds(J0 + own, 1), :], s_j_in.at[:, :, pl.ds(other, 1), :]
            device = j_side[side][1]
        return remote(src, dst, s_send.at[axis, side], s_recv.at[axis, 1 - side], device)

    def on_sides(sides, make, act):
        for side in (0, 1):

            @pl.when(sides[side][0])
            def _():
                act(make, side)

    def start(make, side):
        make(side).start()

    def arrived(make, side):
        make(1 - side).wait_recv()

    def sent(make, side):
        make(side).wait_send()

    load_flow.wait()

    def speeds(i):
        density = flow[0, i]
        momentum = flow[1, i] * flow[1, i] + flow[2, i] * flow[2, i] + flow[3, i] * flow[3, i]
        quarter = 0.25 * (jnp.sqrt(momentum) / density + jnp.sqrt(1.4 * flow[4, i] / density))
        for c in range(chunks):
            speed[i + 1, c, rows, :] = quarter[:, 128 * c : 128 * c + 128]

    def loop_speeds(first, count, stride):
        def step(t, carry):
            speeds(first + stride * t)
            return carry

        lax.fori_loop(0, count, step, 0)

    loop_speeds(0, ni, 1)
    for copy in load_start:
        copy.wait()

    peers = sum(len(stage) for stage in stages)
    for there, _ in i_side + j_side:
        peers = peers + jnp.where(there, 1, 0)
    pl.semaphore_wait(barrier, peers)

    on_sides(j_side, lambda side: halo_j(0, 0, side, 0, ni), start)
    on_sides(j_side, functools.partial(halo_speed, 1), start)
    on_sides(i_side, functools.partial(halo_speed, 0), start)
    for c in range(chunks):
        on_sides(i_side, lambda side: halo_i(0, side, c, 1), start)

    zero_plane = jnp.zeros((chunks, nj, 128), jnp.float32)
    zero_row = jnp.zeros((1, 128), jnp.float32)
    for plane in (0, ni + 1):
        speed[plane, :, rows, :] = zero_plane
        for u in range(NV):
            v0[u, plane, :, rows, :] = zero_plane
            v1[u, plane, :, rows, :] = zero_plane

    def clear_beside(i, carry):
        for c in range(chunks):
            for row in (J0 - 1, J0 + nj):
                speed[i + 1, c, pl.ds(row, 1), :] = zero_row
                for u in range(NV):
                    v0[u, i + 1, c, pl.ds(row, 1), :] = zero_row
                    v1[u, i + 1, c, pl.ds(row, 1), :] = zero_row
        return carry

    lax.fori_loop(0, ni, clear_beside, 0)
    for side in (0, 1):

        @pl.when(jnp.logical_not(i_side[side][0]))
        def _():
            s_i_in[side] = zero_plane
            for u in range(NV):
                i_in[0, side, u] = zero_plane
                i_in[1, side, u] = zero_plane

        @pl.when(jnp.logical_not(j_side[side][0]))
        def _():
            row = 0 if side == 0 else nj - 1

            def clear(i, carry):
                for c in range(chunks):
                    s_j_in[i, c, pl.ds(row, 1), :] = zero_row
                    for u in range(NV):
                        j_in[0, u, i, c, pl.ds(row, 1), :] = zero_row
                        j_in[1, u, i, c, pl.ds(row, 1), :] = zero_row
                return carry

            lax.fori_loop(0, ni, clear, 0)

    lane = lax.broadcasted_iota(jnp.int32, (nj, 128), 1)
    diagonal = lax.broadcasted_iota(jnp.int32, (nj, nj), 0) == lax.broadcasted_iota(jnp.int32, (nj, nj), 1)
    load_codes.wait()
    for i in range(ni):
        line = jnp.broadcast_to(codes[i : i + 1, :].astype(jnp.float32), (nj, nj))
        column = jnp.sum(jnp.where(diagonal, line, 0.0), axis=1, keepdims=True)
        column = jnp.broadcast_to(column, (nj, 128))
        ghost[i] = jnp.where(column == 1.0, 0.0, -1.0)
        flip[i] = jnp.where((column == 0.0) & (lane == 0), 2.0, 0.0)

    load_jac.wait()
    half = [[[0.5 * jac[u, d, v] for v in range(NV)] for u in range(NV)] for d in range(3)]

    def along_k(read, h, mirror):
        own = [read(2 * h), read(2 * h + 1)]
        up = [pltpu.roll(x, 1, 1) for x in own]
        down = [pltpu.roll(x, 127, 1) for x in own]
        before = mirror * own[0] if h == 0 else pltpu.roll(read(2 * h - 1), 1, 1)
        after = jnp.zeros_like(own[0]) if 2 * h + 2 == chunks else pltpu.roll(read(2 * h + 2), 127, 1)
        first, last = lane == 0, lane == 127
        left = [jnp.where(first, before, up[0]), jnp.where(first, up[0], up[1])]
        right = [jnp.where(last, down[1], down[0]), jnp.where(last, after, down[1])]
        return own, left, right

    def inside(v, i, h):
        mirror = ghost[i]
        s_own, s_left, s_right = along_k(lambda c: speed[i + 1, c, rows, :], h, mirror)
        around = [along_k(lambda c, u=u: v[u, i + 1, c, rows, :], h, mirror) for u in range(NV)]
        for q in (0, 1):
            c = 2 * h + q
            own = [around[u][0][q] for u in range(NV)]
            s = s_own[q]
            places = [
                (speed[i, c, rows, :], lambda u, c=c: v[u, i, c, rows, :]),
                (speed[i + 2, c, rows, :], lambda u, c=c: v[u, i + 2, c, rows, :]),
                (speed[i + 1, c, pl.ds(J0 - 1, nj), :], lambda u, c=c: v[u, i + 1, c, pl.ds(J0 - 1, nj), :]),
                (speed[i + 1, c, pl.ds(J0 + 1, nj), :], lambda u, c=c: v[u, i + 1, c, pl.ds(J0 + 1, nj), :]),
                (s_left[q], lambda u, q=q: around[u][1][q]),
                (s_right[q], lambda u, q=q: around[u][2][q]),
            ]
            weights = [s + beside for beside, _ in places]
            total = functools.reduce(jnp.add, weights)
            r = [source[u, i, :, 128 * c : 128 * c + 128] - total * own[u] for u in range(NV)]
            for d in range(3):
                jump = []
                for u in range(NV):
                    low, high = places[2 * d][1](u), places[2 * d + 1][1](u)
                    r[u] = r[u] + (weights[2 * d] * low + weights[2 * d + 1] * high)
                    jump.append(high - low)
                for w in range(NV):
                    for u in range(NV):
                        r[w] = r[w] + half[d][u][w] * jump[u]
            if c == 0:
                wall = s * own[3]
                for u in range(NV):
                    wall = wall + half[2][u][3] * own[u]
                r[3] = r[3] - flip[i] * wall
            for u in range(NV):
                residual[u, i, c] = r[u]

    row = lax.broadcasted_iota(jnp.int32, (nj, 128), 0)
    edge = (row == 0) | (row == nj - 1)
    edge_sign = jnp.where(row < nj // 2, -1.0, 1.0)

    def add_beside(r, s, own, s_beside, beside, d, sign):
        weight = s + s_beside
        signed = [sign * x for x in beside]
        for w in range(NV):
            r[w] = r[w] + (weight * beside[w] - s_beside * own[w])
            for u in range(NV):
                r[w] = r[w] + half[d][u][w] * signed[u]

    def whole(v, sweep, i, c, side):
        r = [residual[u, i, c] for u in range(NV)]
        s = speed[i + 1, c, rows, :]
        own = [v[u, i + 1, c, rows, :] for u in range(NV)]
        beside = [jnp.where(edge, j_in[sweep, u, i, c], 0.0) for u in range(NV)]
        add_beside(r, s, own, jnp.where(edge, s_j_in[i, c], 0.0), beside, 1, edge_sign)
        if side is not None:
            beside = [i_in[sweep, side, u, c] for u in range(NV)]
            add_beside(r, s, own, s_i_in[side, c], beside, 0, (2 * side - 1).astype(jnp.float32))
        return r, own

    def preconditioned(r, own, i, c):
        new = []
        for w in range(NV):
            total = own[w]
            for u in range(NV):
                total = total + precond[u, w, i, :, 128 * c : 128 * c + 128] * r[u]
            new.append(total)
        return new

    def first_sweep(i, c, side, squares):
        r, own = whole(v0, 0, i, c, side)
        for w, new in enumerate(preconditioned(r, own, i, c)):
            v1[w, i + 1, c, rows, :] = new
        return squares + functools.reduce(jnp.add, [x * x for x in r])

    def second_sweep(i, c, side, squares):
        r, _ = whole(v1, 1, i, c, side)
        for u in range(NV):
            residual[u, i, c] = r[u]
        return squares + functools.reduce(jnp.add, [x * x for x in r])

    def all_inside(v):
        def step(i, carry):
            for h in halves:
                inside(v, i, h)
            return carry

        lax.fori_loop(0, ni, step, 0)

    def inner_planes(act, squares, first, end):
        def step(i, carry):
            for c in range(chunks):
                carry = act(i, c, None, carry)
            return carry

        return lax.fori_loop(first, end, step, squares)

    def outer_planes(act, h, squares):
        def step(side, carry):
            for c in (2 * h, 2 * h + 1):
                carry = act((ni - 1) * side, c, side, carry)
            return carry

        return lax.fori_loop(0, 2, step, squares)

    none = jnp.zeros((nj, 128), jnp.float32)
    halves = tuple(range(chunks // 2))

    outer_j = [lambda side: halo_j(1, 2, side, 0, 1), lambda side: halo_j(1, 3, side, ni - 1, 1)]

    load_source.wait()
    all_inside(v0)
    for copy in load_precond:
        copy.wait()
    on_sides(j_side, functools.partial(halo_speed, 1), arrived)
    on_sides(j_side, lambda side: halo_j(0, 0, side, 0, ni), arrived)
    low = ni // 2 - 1
    inner_j = [lambda side: halo_j(1, 1, side, 1, low), lambda side: halo_j(1, 4, side, 1 + low, ni - 2 - low)]
    squares0 = inner_planes(first_sweep, none, 1, 1 + low)
    on_sides(j_side, inner_j[0], start)
    squares0 = inner_planes(first_sweep, squares0, 1 + low, ni - 1)
    on_sides(j_side, inner_j[1], start)
    on_sides(i_side, functools.partial(halo_speed, 0), arrived)
    for h in halves:
        for c in (2 * h, 2 * h + 1):
            on_sides(i_side, lambda side: halo_i(0, side, c, 1), arrived)
        squares0 = outer_planes(first_sweep, h, squares0)
        if h == halves[-1]:
            for make in outer_j:
                on_sides(j_side, make, start)
        on_sides(i_side, lambda side: halo_i(1, side, 2 * h, 2), start)

    all_inside(v1)
    squares1 = none
    for make, first, end in zip(inner_j, (1, 1 + low), (1 + low, ni - 1)):
        on_sides(j_side, make, arrived)
        squares1 = inner_planes(second_sweep, squares1, first, end)
    for make in outer_j:
        on_sides(j_side, make, arrived)
    for h in halves:
        on_sides(i_side, lambda side: halo_i(1, side, 2 * h, 2), arrived)
        squares1 = outer_planes(second_sweep, h, squares1)

    def last(i, carry):
        for c in range(chunks):
            r = [residual[u, i, c] for u in range(NV)]
            own = [v1[u, i + 1, c, rows, :] for u in range(NV)]
            for w, new in enumerate(preconditioned(r, own, i, c)):
                out[w, i, :, 128 * c : 128 * c + 128] = new
        return carry

    line = lax.broadcasted_iota(jnp.int32, (8, 128), 0)
    sums = jnp.where(
        line == 0,
        jnp.sum(squares0, axis=0, keepdims=True),
        jnp.where(line == 1, jnp.sum(squares1, axis=0, keepdims=True), 0.0),
    )
    reduction = []
    slot = 0
    for number, stage in enumerate(stages):
        part[number] = sums
        copies = []
        for device in stage:
            copy = pltpu.make_async_remote_copy(
                src_ref=part.at[number], dst_ref=gathered.at[slot], send_sem=r_send.at[slot],
                recv_sem=r_recv.at[slot], device_id=device, device_id_type=MESH,
            )
            copy.start()
            copies.append((slot, copy))
            slot += 1
        if number == 0:
            lax.fori_loop(0, ni, last, 0)
        for where, copy in copies:
            copy.wait_recv()
            sums = sums + gathered[where]
        reduction += [copy for _, copy in copies]
    sums_ref[...] = sums

    for copy in reduction:
        copy.wait_send()
    for c in range(chunks):
        on_sides(i_side, lambda side: halo_i(0, side, c, 1), sent)
    for h in halves:
        on_sides(i_side, lambda side: halo_i(1, side, 2 * h, 2), sent)
    on_sides(j_side, lambda side: halo_j(0, 0, side, 0, ni), sent)
    for make in [*inner_j, *outer_j]:
        on_sides(j_side, make, sent)
    on_sides(i_side, functools.partial(halo_speed, 0), sent)
    on_sides(j_side, functools.partial(halo_speed, 1), sent)


def deliver(cells_all, adjoint_vmem, sums_ref, adjoint_ref, rms_ref, sem):
    copy = pltpu.make_async_copy(adjoint_vmem, adjoint_ref, sem)
    copy.start()
    root = jnp.sqrt(jnp.sum(sums_ref[...], axis=1, keepdims=True) / cells_all)
    rms_ref[0] = root[0, 0]
    rms_ref[1] = root[1, 0]
    copy.wait()


def per_device(adjoint_start, source, flow_state, precond, flux_jac, bc_codes):
    nv, ni, nj, nk = adjoint_start.shape
    cells_all = float(adjoint_start.size * lax.axis_size("stream") * lax.axis_size("span"))
    block = (ni, nk // 128, nj, 128)
    padded = (ni + 2, nk // 128, nj + 2 * J0, 128)
    hbm, vmem = pl.BlockSpec(memory_space=pltpu.HBM), pl.BlockSpec(memory_space=pltpu.VMEM)
    in_hbm = functools.partial(pltpu.with_memory_space_constraint, memory_space=pltpu.HBM)
    dma = pltpu.SemaphoreType.DMA
    adjoint, sums = pl.pallas_call(
        kernel,
        out_shape=(
            pltpu.VMEM(adjoint_start.shape, jnp.float32),
            pltpu.VMEM((8, 128), jnp.float32),
        ),
        in_specs=[hbm, hbm, hbm, hbm, hbm, hbm],
        out_specs=(vmem, vmem),
        scratch_shapes=[
            pltpu.VMEM((nv, *padded), jnp.float32),
            pltpu.VMEM((nv, *padded), jnp.float32),
            pltpu.VMEM(padded, jnp.float32),
            pltpu.VMEM((2, 2, nv, nk // 128, nj, 128), jnp.float32),
            pltpu.VMEM((2, nv, *block), jnp.float32),
            pltpu.VMEM((2, nk // 128, nj, 128), jnp.float32),
            pltpu.VMEM(block, jnp.float32),
            pltpu.VMEM((nv, *block), jnp.float32),
            pltpu.VMEM(flow_state.shape, jnp.float32),
            pltpu.VMEM(source.shape, jnp.float32),
            pltpu.VMEM(precond.shape, jnp.float32),
            pltpu.SMEM((nv, 3, nv), jnp.float32),
            pltpu.VMEM(bc_codes.shape, jnp.int32),
            pltpu.VMEM((ni, nj, 128), jnp.float32),
            pltpu.VMEM((ni, nj, 128), jnp.float32),
            pltpu.VMEM((2, 8, 128), jnp.float32),
            pltpu.VMEM((30, 8, 128), jnp.float32),
            dma((16,)),
            dma((2, 2, nk // 128)),
            dma((2, 2, nk // 128)),
            dma((5, 2)),
            dma((5, 2)),
            dma((2, 2)),
            dma((2, 2)),
            dma((30,)),
            dma((30,)),
        ],
        compiler_params=pltpu.CompilerParams(
            collective_id=0, has_side_effects=True, vmem_limit_bytes=40 * 1024 * 1024
        ),
        cost_estimate=pl.CostEstimate(flops=40_000_000, bytes_accessed=13_000_000, transcendentals=131072),
        name="jacobi_sweeps",
    )(*map(in_hbm, (adjoint_start, source, flow_state, precond, jnp.transpose(flux_jac, (1, 0, 2)), bc_codes)))
    return pl.pallas_call(
        functools.partial(deliver, cells_all),
        out_shape=(
            jax.ShapeDtypeStruct(adjoint.shape, jnp.float32),
            jax.ShapeDtypeStruct((2,), jnp.float32),
        ),
        in_specs=[vmem, vmem],
        out_specs=(hbm, pl.BlockSpec(memory_space=pltpu.SMEM)),
        scratch_shapes=[dma],
        compiler_params=pltpu.CompilerParams(vmem_limit_bytes=4 * 1024 * 1024),
        name="deliver",
    )(*(pltpu.with_memory_space_constraint(x, memory_space=pltpu.VMEM) for x in (adjoint, sums)))


def solution(mesh):
    split = P(None, "stream", "span", None)
    return jax.shard_map(
        per_device,
        mesh=mesh,
        in_specs=(split, split, split, P(None, None, "stream", "span", None), P(), P("stream", "span")),
        out_specs=(split, P()),
        check_vma=False,
    )
```
